32 devices in a mesh: groups: 2 (over x), tensor: 16 (over z, y, core).
Axes of the slice: x: 2, y: 2, z: 4, core: 2. Of those that a mesh axis runs over, the one named last changes fastest.
Arguments:
- hidden_in: bfloat16 [7, 4096, 1024], P(None, 'tensor', 'groups'), parts along dimension 2, may hold values from -6 to 6
- out_grad: bfloat16 [1024, 8192], P('groups'), parts along dimension 0, may hold values from -6 to 6
- down_weight: bfloat16 [7, 4096, 8192], P(None, 'tensor'), may hold values from -0.03125 to 0.03125
- hidden_signs: int32 [3, 7, 4096], replicated, may hold values 0 or 1
- grad_signs: int32 [3, 8192], replicated, may hold values 0 or 1
- hidden_picks: int32 [64], replicated, may hold values from 0 to 28671
- grad_picks: int32 [64], replicated, may hold values from 0 to 8191
- seq_lengths: int32 [16], P('groups'), parts along dimension 0, may hold values from 16 to 64, as said below
Outputs:
- input_grad: bfloat16 [7, 4096, 1024], P(None, 'tensor', 'groups'), parts along dimension 2
- example_sketch: float32 [16, 4096], P('groups', 'tensor'), parts along dimension 0
The draws below stay inside these ranges and needn't reach their ends.
There are 2 independent parts, one for each index of `groups`. The reference program is written for one: setup_inputs(seed, part) draws one part's arguments, and reference() takes and returns one part's arrays. A program takes and returns all parts, laid end to end along the dimension named above; an argument that names none is the same for every part. Nothing has to cross between parts.
Inputs may be any that keep to these rules, and one draw needn't show every extreme that they name: `hidden_picks`: a flat hidden unit index q * 4096 + r. `seq_lengths`: live tokens stand at the start of each sequence; in every draw some sequence is full and some has 16.
All inputs are finite; a program needn't handle non-finite values.
Results may differ from the reference program's by a relative error of at most 0.001.
Values may be sent and summed in bfloat16 or wider, within the bound.
A program may use at most 192 MiB of HBM per device.

```python
import math
import jax
import jax.numpy as jnp
from jax import lax

D = 8192
FQ = 7
FB = 4096
FF = 28672
K = 64
SEQS = 8
SEQLEN = 64
TOKENS = 512


def draw_seq_lengths(key, part):
    key = jax.random.fold_in(key, 5)
    first_key, second_key = jax.random.split(key)
    drawn = jax.random.randint(first_key, (SEQS,), SEQLEN // 4, SEQLEN + 1)
    order = jax.random.permutation(second_key, SEQS)
    drawn = drawn.at[order[0]].set(SEQLEN)
    drawn = drawn.at[order[1]].set(SEQLEN // 4)
    return drawn.astype(jnp.int32)


def plant(values, rng, smallest, top_value):
    spot = [jax.random.randint(jax.random.fold_in(rng, axis), (), 0, length) for axis, length in enumerate(values.shape)]
    main_axis = values.shape.index(max(values.shape))
    next_to = spot[:main_axis] + [(spot[main_axis] + 1) % values.shape[main_axis]] + spot[main_axis + 1:]
    return values.at[tuple(spot)].set(smallest).at[tuple(next_to)].set(top_value)


def block_scale(stream_key, dims, cuts, low, largest):
    def one(axis_at, parts):
        heights = jax.random.uniform(jax.random.fold_in(jax.random.fold_in(stream_key, 6), axis_at), (parts,), jnp.float32, low / len(cuts), largest / len(cuts))
        return jnp.repeat(jnp.exp(heights), dims[axis_at] // parts).reshape((-1,) + (1,) * (len(dims) - axis_at - 1))

    loudness = one(*cuts[0])
    for cut in cuts[1:]:
        loudness = loudness * one(*cut)
    return loudness


def centred(key, extent, scale, bound, cuts=(), kind=jnp.bfloat16):
    result = scale * jax.random.normal(key, extent, jnp.float32)
    if cuts:
        result = result * block_scale(key, extent, cuts, -0.22, 0.18)
    return jnp.clip(result, -bound, bound).astype(kind)


def setup_inputs(seed: int = 0, part: int = 0) -> dict:
    seeds = jax.random.split(jax.random.key(seed), 9)
    part_splits = jax.random.split(jax.random.fold_in(seeds[8], part), 9)
    hidden_in = centred(part_splits[0], (FQ, FB, TOKENS), 0.5, 6.0, ((1, 16),))
    out_grad = centred(part_splits[1], (TOKENS, D), 1.0, 6.0)
    down_weight = centred(seeds[2], (FQ, FB, D), FF ** -0.5, 0.03125, ((1, 16),))
    hidden_signs = plant((jax.random.randint(seeds[3], (3, FQ, FB), 0, 2) < 1).astype(jnp.int32), jax.random.fold_in(seeds[3], 1), 0, 1)
    grad_signs = plant((jax.random.randint(seeds[4], (3, D), 0, 2) < 1).astype(jnp.int32), jax.random.fold_in(seeds[4], 1), 0, 1)
    hidden_picks = plant(jax.random.randint(seeds[5], (K,), 0, FF), jax.random.fold_in(seeds[5], 1), 0, FF - 1).astype(jnp.int32)
    grad_picks = plant(jax.random.randint(seeds[6], (K,), 0, D), jax.random.fold_in(seeds[6], 1), 0, D - 1).astype(jnp.int32)
    seq_lengths = draw_seq_lengths(jax.random.fold_in(jax.random.fold_in(seeds[8], part), 71), part)
    return dict(hidden_in=hidden_in, out_grad=out_grad, down_weight=down_weight, hidden_signs=hidden_signs, grad_signs=grad_signs, hidden_picks=hidden_picks, grad_picks=grad_picks, seq_lengths=seq_lengths)


highest = lax.Precision.HIGHEST

def parity_sign(first_ids, second_ids):
    parity_sum = jnp.zeros_like(first_ids + second_ids)
    for position in range(16):
        step_size = 2 ** position
        parity_sum = parity_sum + first_ids // step_size % 2 * (second_ids // step_size % 2)
    return (1 - 2 * (parity_sum % 2)).astype(jnp.float32)

def walsh_table(length):
    indices = jnp.arange(length, dtype=jnp.int32)
    return parity_sign(indices[:, None], indices[None, :])

def split_length(length):
    bits_count = length.bit_length() - 1
    first_len = 2 ** (bits_count // 2)
    return (first_len, length // first_len)

def walsh_middle(values, length):
    first_len, second_len = split_length(length)
    shaped = values.reshape(values.shape[0], first_len, second_len, values.shape[2])
    shaped = jnp.einsum('ac,qcbt->qabt', walsh_table(first_len), shaped, precision=highest)
    shaped = jnp.einsum('bd,qadt->qabt', walsh_table(second_len), shaped, precision=highest)
    return shaped.reshape(values.shape) / math.sqrt(length)

def walsh_last(values, length):
    first_len, second_len = split_length(length)
    shaped = values.reshape(values.shape[0], first_len, second_len)
    shaped = jnp.einsum('ac,ncb->nab', walsh_table(first_len), shaped, precision=highest)
    shaped = jnp.einsum('bd,nad->nab', walsh_table(second_len), shaped, precision=highest)
    return shaped.reshape(values.shape) / math.sqrt(length)

def reference(hidden_in, out_grad, down_weight, hidden_signs, grad_signs, hidden_picks, grad_picks, seq_lengths):
    flat_weight = down_weight.reshape(FQ * FB, D)
    input_grad = jnp.dot(flat_weight, out_grad.T, preferred_element_type=jnp.float32)
    input_grad = input_grad.astype(jnp.bfloat16).reshape(FQ, FB, TOKENS)
    hidden_sign = (1 - 2 * hidden_signs).astype(jnp.float32)
    mixed = hidden_in.astype(jnp.float32)
    for section_num in range(3):
        mixed = walsh_middle(mixed * hidden_sign[section_num][:, :, None], FB)
    hidden_proj = mixed.reshape(FQ * FB, TOKENS)[hidden_picks]
    grad_sign = (1 - 2 * grad_signs).astype(jnp.float32)
    mixed_grad = out_grad.astype(jnp.float32)
    for section_num in range(3):
        mixed_grad = walsh_last(mixed_grad * grad_sign[section_num][None, :], D)
    grad_proj = mixed_grad[:, grad_picks]
    positions = jnp.arange(TOKENS, dtype=jnp.int32)
    owner_seq = positions // SEQLEN
    seq_ids = jnp.arange(SEQS, dtype=jnp.int32)
    live_mask = ((owner_seq[None, :] == seq_ids[:, None]) & ((positions % SEQLEN)[None, :] < seq_lengths[:, None])).astype(jnp.float32)
    weighted = live_mask[:, None, :] * hidden_proj[None, :, :]
    example_sketch = jnp.einsum('skt,tb->skb', weighted, grad_proj, precision=highest).reshape(SEQS, K * K)
    return (input_grad, example_sketch)
```

```python
import functools
import math

import jax
import jax.numpy as jnp
from jax import lax
from jax.experimental import pallas as pl
from jax.experimental.pallas import tpu as pltpu
from jax.sharding import PartitionSpec as P

highest = lax.Precision.HIGHEST
MB = 1 << 20
BLOCK = 256
BF, F32 = jnp.bfloat16, jnp.float32


def parity_sign(first_ids, second_ids):
    common = first_ids & second_ids
    for shift in (8, 4, 2, 1):
        common = common ^ (common >> shift)
    return (1 - 2 * (common & 1)).astype(F32)


def iota(shape, dim):
    return lax.broadcasted_iota(jnp.int32, shape, dim)


def table():
    return parity_sign(iota((BLOCK, BLOCK), 0), iota((BLOCK, BLOCK), 1)).astype(BF)


def dot(a, b):
    return jnp.dot(a, b, preferred_element_type=F32)


def dot_nt(a, b):
    return lax.dot_general(a, b, (((1,), (1,)), ((), ())), preferred_element_type=F32)


def two_terms(x):
    hi = x.astype(BF)
    return hi, (x - hi.astype(F32)).astype(BF)


def butterflies(blocks):
    blocks = list(blocks)
    step = 1
    while step < len(blocks):
        for i in range(len(blocks)):
            if not i & step:
                a, b = blocks[i], blocks[i + step]
                blocks[i], blocks[i + step] = a + b, a - b
        step *= 2
    return blocks


def hidden_kernel(n, picks_ref, signs_ref, x_ref, out_ref):
    blocks, rows, _ = x_ref.shape
    length = signs_ref.shape[2]
    parts = length // BLOCK
    sketch = picks_ref.shape[0]
    start = lax.axis_index("tensor") * rows
    home = start // BLOCK
    picks = picks_ref[...]
    pick_q = picks // length
    pick_r = picks % length
    chosen = (pick_q == iota((sketch, blocks), 1)).astype(BF)

    def sign_of(section, where):
        return 1.0 - 2.0 * dot(chosen, signs_ref[section, :, where].astype(F32).astype(BF))

    walsh = table()
    low = parity_sign(pick_r % BLOCK, iota((sketch, BLOCK), 1))
    high = pick_r // BLOCK
    first = []
    for c in range(parts):
        where = pl.ds(c * BLOCK, BLOCK)
        v = low * parity_sign(high, jnp.full_like(high, c)) * sign_of(2, where)
        first.append(dot(v.astype(BF), walsh))
    first = butterflies(first)
    total = None
    for c in range(parts):
        side = parity_sign(jnp.full((1, BLOCK), home, jnp.int32), jnp.full((1, BLOCK), c, jnp.int32))
        term = first[c] * (sign_of(1, pl.ds(c * BLOCK, BLOCK)) * side)
        total = term if total is None else total + term
    hi, lo = two_terms(total)
    second = dot(hi, walsh) + dot(lo, walsh)
    second = second * sign_of(0, pl.ds(pl.multiple_of(home * BLOCK, BLOCK), BLOCK))
    hi, lo = two_terms(second)
    if rows < BLOCK:
        pick_out = (iota((BLOCK, rows), 0) == iota((BLOCK, rows), 1) + (start - home * BLOCK)).astype(F32).astype(BF)
        hi = dot(hi, pick_out).astype(BF)
        lo = dot(lo, pick_out).astype(BF)
    total = None
    for q in range(blocks):
        own = pick_q == q
        both = jnp.concatenate([jnp.where(own, hi.astype(F32), 0.0), jnp.where(own, lo.astype(F32), 0.0)], axis=0)
        term = dot(both.astype(BF), x_ref[q])
        total = term if total is None else total + term
    out_ref[...] = (total[:sketch] + total[sketch:]) * (length ** -1.5)


def main_kernel(steps, picks_ref, signs_ref, w_ref, g_hbm, out_ref, proj_ref, g_vm, acc, sketcher, sems):
    i = pl.program_id(0)
    width = g_hbm.shape[1]
    tile = width // steps
    parts = width // BLOCK

    def fetch(j):
        return pltpu.make_async_copy(
            g_hbm.at[:, pl.ds(pl.multiple_of(j * tile, tile), tile)], g_vm.at[j], sems.at[j]
        )

    @pl.when(i == 0)
    def _():
        fetch(0).start()
        acc[...] = jnp.zeros_like(acc)

    @pl.when(i < steps - 1)
    def _():
        fetch(i + 1).start()

    fetch(i).wait()
    picks = picks_ref[pl.ds(pl.multiple_of(i * 8, 8), 8), :]
    walsh = table()
    low = parity_sign(picks % BLOCK, iota((8, BLOCK), 1))
    high = picks // BLOCK

    def sign_of(section, c):
        bits = signs_ref[section : section + 1, c * BLOCK : (c + 1) * BLOCK]
        return (1 - 2 * bits).astype(F32)

    def rows_of(x, c):
        return x[c * 8 : (c + 1) * 8]

    v = [low * parity_sign(high, jnp.full_like(high, c)) * sign_of(2, c) for c in range(parts)]
    first = dot(jnp.concatenate(v, axis=0).astype(BF), walsh)
    first = butterflies([rows_of(first, c) for c in range(parts)])
    first = jnp.concatenate([first[c] * sign_of(1, c) for c in range(parts)], axis=0)
    hi, lo = two_terms(first)
    second = dot(hi, walsh) + dot(lo, walsh)
    second = butterflies([rows_of(second, c) for c in range(parts)])
    for c in range(parts):
        x = second[c] * sign_of(0, c)
        h = x.astype(BF).astype(F32)
        both = jnp.concatenate([h, x - h], axis=0).astype(BF)
        at = c * BLOCK // tile
        sketcher[at, pl.ds(pl.multiple_of(i * 16, 16), 16), c * BLOCK - at * tile : (c + 1) * BLOCK - at * tile] = both
    acc[...] += dot_nt(w_ref[...], g_vm[i])

    @pl.when(i == steps - 1)
    def _():
        out_ref[...] = acc[...].astype(BF)
        total = dot_nt(sketcher[0], g_vm[0])
        for j in range(1, steps):
            total = total + dot_nt(sketcher[j], g_vm[j])
        for j in range(steps):
            proj_ref[j * 8 : (j + 1) * 8, :] = (total[j * 16 : j * 16 + 8] + total[j * 16 + 8 : j * 16 + 16]) * (
                width ** -1.5
            )


def make_mask(positions, seq_lengths, seq_len):
    owner_seq = positions // seq_len
    seq_ids = jnp.arange(seq_lengths.shape[0], dtype=jnp.int32)
    inside = (positions % seq_len)[None, :] < seq_lengths[:, None]
    return ((owner_seq[None, :] == seq_ids[:, None]) & inside).astype(F32)


def body(hidden_in, out_grad, down_weight, hidden_signs, grad_signs, hidden_picks, grad_picks, seq_lengths):
    n = lax.axis_size("tensor")
    rank = lax.axis_index("tensor")
    blocks, rows, tokens = hidden_in.shape
    width = out_grad.shape[1]
    sketch = hidden_picks.shape[0]
    seqs = seq_lengths.shape[0]
    seq_len = tokens // seqs
    vmem = pl.BlockSpec(memory_space=pltpu.VMEM)
    partial = pl.pallas_call(
        functools.partial(hidden_kernel, n),
        out_shape=jax.ShapeDtypeStruct((sketch, tokens), F32),
        in_specs=[vmem] * 3,
        out_specs=vmem,
        compiler_params=pltpu.CompilerParams(vmem_limit_bytes=32 * MB),
        cost_estimate=pl.CostEstimate(flops=10**9, bytes_accessed=4 * 10**6, transcendentals=0),
    )(hidden_picks.reshape(sketch, 1), hidden_signs, hidden_in)
    scatter = sketch % n == 0
    if scatter:
        hidden_proj = lax.psum_scatter(partial, "tensor", scatter_dimension=0, tiled=True)
    else:
        hidden_proj = lax.psum(partial, "tensor")

    steps = sketch // 8
    tile = width // steps
    m = blocks * rows
    flat_weight = down_weight.reshape(m, width)
    input_grad, grad_proj = pl.pallas_call(
        functools.partial(main_kernel, steps),
        grid=(steps,),
        out_shape=(jax.ShapeDtypeStruct((m, tokens), BF), jax.ShapeDtypeStruct((sketch, tokens), F32)),
        in_specs=[
            pl.BlockSpec((sketch, 1), lambda i: (0, 0)),
            pl.BlockSpec(grad_signs.shape, lambda i: (0, 0)),
            pl.BlockSpec((m, tile), lambda i: (0, i)),
            pl.BlockSpec(memory_space=pl.ANY),
        ],
        out_specs=(pl.BlockSpec((m, tokens), lambda i: (0, 0)), pl.BlockSpec((sketch, tokens), lambda i: (0, 0))),
        scratch_shapes=[
            pltpu.VMEM((steps, tokens, tile), BF),
            pltpu.VMEM((m, tokens), F32),
            pltpu.VMEM((steps, 2 * sketch, tile), BF),
            pltpu.SemaphoreType.DMA((steps,)),
        ],
        compiler_params=pltpu.CompilerParams(vmem_limit_bytes=48 * MB, dimension_semantics=("arbitrary",)),
        cost_estimate=pl.CostEstimate(
            flops=2 * (m + 2 * sketch) * tokens * width, bytes_accessed=2 * (m + tokens) * width, transcendentals=0
        ),
    )(grad_picks.reshape(sketch, 1), grad_signs, flat_weight, out_grad)
    input_grad = input_grad.reshape(blocks, rows, tokens)

    share = sketch * sketch // n
    live = make_mask(jnp.arange(tokens, dtype=jnp.int32), seq_lengths, seq_len)
    live = live.reshape(seqs, seqs, seq_len).sum(axis=0)
    left = hidden_proj.reshape(-1, seqs, seq_len) * live[None]
    right = grad_proj.reshape(sketch, seqs, seq_len)
    found = jnp.einsum("ast,bst->sab", left, right, precision=highest).reshape(seqs, -1)
    if not scatter:
        found = lax.dynamic_slice_in_dim(found, rank * share, share, 1)
    return (input_grad, found)


def solution(mesh):
    in_specs = (
        P(None, "tensor", "groups"),
        P("groups", None),
        P(None, "tensor", None),
        P(),
        P(),
        P(),
        P(),
        P("groups"),
    )
    out_specs = (P(None, "tensor", "groups"), P("groups", "tensor"))
    return jax.shard_map(body, mesh=mesh, in_specs=in_specs, out_specs=out_specs, check_vma=False)
```

```python
import functools

import jax
import jax.numpy as jnp
from jax import lax
from jax.experimental import pallas as pl
from jax.experimental.pallas import tpu as pltpu
from jax.sharding import PartitionSpec as P

highest = lax.Precision.HIGHEST
MB = 1 << 20
BLOCK = 256
BF, F32 = jnp.bfloat16, jnp.float32


def parity_sign(first_ids, second_ids):
    common = first_ids & second_ids
    for shift in (8, 4, 2, 1):
        common = common ^ (common >> shift)
    return (1 - 2 * (common & 1)).astype(F32)


def iota(shape, dim):
    return lax.broadcasted_iota(jnp.int32, shape, dim)


def table():
    return parity_sign(iota((BLOCK, BLOCK), 0), iota((BLOCK, BLOCK), 1)).astype(BF)


def dot(a, b):
    return jnp.dot(a, b, preferred_element_type=F32)


def dot_nt(a, b):
    return lax.dot_general(a, b, (((1,), (1,)), ((), ())), preferred_element_type=F32)


def two_terms(x):
    hi = x.astype(BF)
    return hi, (x - hi.astype(F32)).astype(BF)


def butterflies(blocks):
    blocks = list(blocks)
    step = 1
    while step < len(blocks):
        for i in range(len(blocks)):
            if not i & step:
                a, b = blocks[i], blocks[i + step]
                blocks[i], blocks[i + step] = a + b, a - b
        step *= 2
    return blocks


def column(row, base, count):
    shape = (count, row.shape[1])
    wanted = iota(shape, 1) == iota(shape, 0) + base
    return jnp.sum(jnp.where(wanted, row.astype(F32), 0.0), axis=1, keepdims=True).astype(jnp.int32)


def hidden_share(me, picks, signs_ref, shape):
    blocks, rows, _ = shape
    length = signs_ref.shape[2]
    parts = length // BLOCK
    sketch = picks.shape[0]
    start = me * rows
    home = start // BLOCK
    pick_q = picks // length
    pick_r = picks % length
    chosen = (pick_q == iota((sketch, blocks), 1)).astype(F32).astype(BF)

    def sign_of(section, where):
        return 1.0 - 2.0 * dot(chosen, signs_ref[section, :, where].astype(F32).astype(BF))

    walsh = table()
    low = parity_sign(pick_r % BLOCK, iota((sketch, BLOCK), 1))
    high = pick_r // BLOCK
    first = []
    for c in range(parts):
        v = low * parity_sign(high, jnp.full_like(high, c)) * sign_of(2, pl.ds(c * BLOCK, BLOCK))
        first.append(dot(v.astype(BF), walsh))
    first = butterflies(first)
    total = None
    for c in range(parts):
        side = parity_sign(jnp.full((1, BLOCK), home, jnp.int32), jnp.full((1, BLOCK), c, jnp.int32))
        term = first[c] * (sign_of(1, pl.ds(c * BLOCK, BLOCK)) * side)
        total = term if total is None else total + term
    hi, lo = two_terms(total)
    second = dot(hi, walsh) + dot(lo, walsh)
    second = second * sign_of(0, pl.ds(pl.multiple_of(home * BLOCK, BLOCK), BLOCK))
    hi, lo = two_terms(second)
    if rows < BLOCK:
        pick_out = (iota((BLOCK, rows), 0) == iota((BLOCK, rows), 1) + (start - home * BLOCK)).astype(F32).astype(BF)
        hi = dot(hi, pick_out).astype(BF)
        lo = dot(lo, pick_out).astype(BF)
    return pick_q, hi, lo


def grad_share(picks, signs_ref, write):
    width = signs_ref.shape[1]
    parts = width // BLOCK
    walsh = table()
    low = parity_sign(picks % BLOCK, iota((8, BLOCK), 1))
    high = picks // BLOCK

    def sign_of(section, c):
        bits = signs_ref[section : section + 1, c * BLOCK : (c + 1) * BLOCK]
        return (1 - 2 * bits).astype(F32)

    def rows_of(x, c):
        return x[c * 8 : (c + 1) * 8]

    v = [low * parity_sign(high, jnp.full_like(high, c)) * sign_of(2, c) for c in range(parts)]
    first = dot(jnp.concatenate(v, axis=0).astype(BF), walsh)
    first = butterflies([rows_of(first, c) for c in range(parts)])
    first = jnp.concatenate([first[c] * sign_of(1, c) for c in range(parts)], axis=0)
    hi, lo = two_terms(first)
    second = dot(hi, walsh) + dot(lo, walsh)
    second = butterflies([rows_of(second, c) for c in range(parts)])
    for c in range(parts):
        x = second[c] * sign_of(0, c)
        h = x.astype(BF).astype(F32)
        write(c, jnp.concatenate([h, x - h], axis=0).astype(BF))


def kernel(
    n, keep, hp_ref, gp_ref, len_ref, hs_hbm, gs_hbm, x_hbm, g_hbm, w_hbm, out_hbm, sk_ref,
    hs_vm, gs_vm, x_vm, g_vm, w_first, w_vm, o_vm, part, send, recv, in_sem, g_sem, w_sem, out_sem, send_sem, recv_sem,
):
    me = lax.axis_index("tensor")
    width = g_hbm.shape[1]
    tiles, bm, tokens = o_vm.shape
    blocks = x_hbm.shape[0]
    length = hs_hbm.shape[2]
    sketch = hp_ref.shape[1]
    pieces = sketch // keep
    seqs = len_ref.shape[1]
    seq_len = tokens // seqs
    g_parts = g_sem.shape[0]
    g_rows = tokens // g_parts

    def fetch_w(t, slot):
        where = pl.ds(pl.multiple_of(t * bm, bm), bm)
        return pltpu.make_async_copy(w_hbm.at[where, :], w_vm.at[slot], w_sem.at[slot + 1])

    def put_out(t):
        where = pl.ds(pl.multiple_of(t * bm, bm), bm)
        return pltpu.make_async_copy(o_vm.at[t], out_hbm.at[where, :], out_sem.at[t])

    def send_to(d):
        peer = lax.rem(me + d, n)
        return pltpu.make_async_remote_copy(
            src_ref=send.at[peer * pieces // n],
            dst_ref=recv.at[me],
            send_sem=send_sem.at[d],
            recv_sem=recv_sem.at[me],
            device_id={"tensor": peer},
            device_id_type=pl.DeviceIdType.MESH,
        )

    signs = [
        pltpu.make_async_copy(gs_hbm, gs_vm, in_sem.at[0]),
        pltpu.make_async_copy(hs_hbm, hs_vm, in_sem.at[1]),
    ]
    get_x = pltpu.make_async_copy(x_hbm, x_vm, in_sem.at[2])
    get_g = [
        pltpu.make_async_copy(g_hbm.at[pl.ds(j * g_rows, g_rows), :], g_vm.at[pl.ds(j * g_rows, g_rows), :], g_sem.at[j])
        for j in range(g_parts)
    ]
    get_w = pltpu.make_async_copy(w_hbm.at[pl.ds(0, bm), :], w_first.at[pl.ds(0, bm), :], w_sem.at[0])
    for copy in signs + [get_x] + get_g + [get_w]:
        copy.start()
    for t in range(1, min(3, tiles)):
        fetch_w(t, t - 1).start()

    barrier = pltpu.get_barrier_semaphore()

    def greet(d, carry):
        pl.semaphore_signal(
            barrier, inc=1, device_id={"tensor": lax.rem(me + d, n)}, device_id_type=pl.DeviceIdType.MESH
        )
        return carry

    lax.fori_loop(1, n, greet, 0)

    signs[0].wait()

    def write(c, both):
        w_first[bm : bm + 16, c * BLOCK : (c + 1) * BLOCK] = both

    grad_share(column(gp_ref[...], me * pieces // n * keep, 8), gs_vm, write)
    signs[1].wait()
    pick_q, hi, lo = hidden_share(me, column(hp_ref[...], 0, sketch), hs_vm, x_hbm.shape)
    get_x.wait()
    total = None
    for q in range(blocks):
        own = pick_q == q
        both = jnp.concatenate([jnp.where(own, hi.astype(F32), 0.0), jnp.where(own, lo.astype(F32), 0.0)], axis=0)
        term = dot(both.astype(BF), x_vm[q])
        total = term if total is None else total + term
    part[...] = (total[:sketch] + total[sketch:]) * (length ** -1.5)
    for copy in get_g:
        copy.wait()
    get_w.wait()

    tall = dot_nt(w_first[...], g_vm[...])
    o_vm[0] = tall[:bm].astype(BF)
    put_out(0).start()
    own_grad = (tall[bm : bm + 8] + tall[bm + 8 : bm + 16]) * (width ** -1.5)
    rest = send.shape[1] - 2 * keep
    for p in range(pieces):
        rows = [part[p * keep : (p + 1) * keep, :], own_grad[:keep]]
        if rest:
            rows.append(jnp.zeros((rest, tokens), F32))
        send[p] = jnp.concatenate(rows, axis=0)
    recv[me] = send[me * pieces // n]
    pl.semaphore_wait(barrier, n - 1)

    def start_send(d, carry):
        send_to(d).start()
        return carry

    lax.fori_loop(1, n, start_send, 0)

    def one_tile(t, carry):
        slot = lax.rem(t - 1, 2)
        fetch_w(t, slot).wait()
        o_vm[t] = dot_nt(w_vm[slot], g_vm[...]).astype(BF)
        put_out(t).start()

        @pl.when(t + 2 < tiles)
        def _():
            fetch_w(t + 2, slot).start()

        return carry

    if tiles > 1:
        lax.fori_loop(1, tiles, one_tile, 0)

    def end_send(d, carry):
        send_to(d).wait_send()
        peer = lax.rem(me + d, n)
        pltpu.make_async_remote_copy(
            src_ref=send.at[0],
            dst_ref=recv.at[peer],
            send_sem=send_sem.at[d],
            recv_sem=recv_sem.at[peer],
            device_id={"tensor": peer},
            device_id_type=pl.DeviceIdType.MESH,
        ).wait_recv()
        return carry

    lax.fori_loop(1, n, end_send, 0)
    found = recv[0][:keep]
    for j in range(1, n):
        found = found + recv[j][:keep]
    grads = jnp.concatenate([recv[p * n // pieces][keep : 2 * keep] for p in range(pieces)], axis=0)
    lens = column(len_ref[...], 0, seqs)
    places = iota((seqs, tokens), 1)
    live = ((places // seq_len == iota((seqs, tokens), 0)) & (places % seq_len < lens)).astype(F32)
    left = jnp.concatenate([live * found[a : a + 1] for a in range(keep)], axis=0)
    result = lax.dot_general(
        left, grads, (((1,), (1,)), ((), ())), precision=highest, preferred_element_type=F32
    )
    sk_ref[...] = jnp.concatenate([result[a * seqs : (a + 1) * seqs] for a in range(keep)], axis=1)

    def end_out(t, carry):
        put_out(t).wait()
        return carry

    lax.fori_loop(0, tiles, end_out, 0)


def body(hidden_in, out_grad, down_weight, hidden_signs, grad_signs, hidden_picks, grad_picks, seq_lengths):
    n = lax.axis_size("tensor")
    rank = lax.axis_index("tensor")
    blocks, rows, tokens = hidden_in.shape
    width = out_grad.shape[1]
    sketch = hidden_picks.shape[0]
    seqs = seq_lengths.shape[0]
    share = sketch * sketch // n
    keep = max(1, sketch // n)
    m = blocks * rows
    bm = BLOCK if m % BLOCK == 0 else m
    tiles = m // bm
    message = -(-2 * keep // 8) * 8
    flat_weight = down_weight.reshape(m, width)
    vmem = pl.BlockSpec(memory_space=pltpu.VMEM)
    hbm = pl.BlockSpec(memory_space=pl.ANY)
    dma = pltpu.SemaphoreType.DMA
    input_grad, example_sketch = pl.pallas_call(
        functools.partial(kernel, n, keep),
        out_shape=(
            jax.ShapeDtypeStruct((m, tokens), BF),
            jax.ShapeDtypeStruct((seqs, keep * sketch), F32),
        ),
        in_specs=[vmem] * 3 + [hbm] * 5,
        out_specs=(hbm, vmem),
        scratch_shapes=[
            pltpu.VMEM(hidden_signs.shape, jnp.int32),
            pltpu.VMEM(grad_signs.shape, jnp.int32),
            pltpu.VMEM(hidden_in.shape, BF),
            pltpu.VMEM((tokens, width), BF),
            pltpu.VMEM((bm + 16, width), BF),
            pltpu.VMEM((2, bm, width), BF),
            pltpu.VMEM((tiles, bm, tokens), BF),
            pltpu.VMEM((sketch, tokens), F32),
            pltpu.VMEM((sketch // keep, message, tokens), F32),
            pltpu.VMEM((n, message, tokens), F32),
            dma((3,)),
            dma((4,)),
            dma((3,)),
            dma((tiles,)),
            dma((n,)),
            dma((n,)),
        ],
        compiler_params=pltpu.CompilerParams(
            vmem_limit_bytes=56 * MB, collective_id=0, has_side_effects=True
        ),
        cost_estimate=pl.CostEstimate(
            flops=2 * m * tokens * width, bytes_accessed=2 * (m + tokens) * width, transcendentals=0
        ),
    )(
        hidden_picks.reshape(1, sketch),
        grad_picks.reshape(1, sketch),
        seq_lengths.reshape(1, seqs),
        hidden_signs,
        grad_signs,
        hidden_in,
        out_grad,
        flat_weight,
    )
    if share < keep * sketch:
        example_sketch = lax.dynamic_slice_in_dim(example_sketch, rank * share % sketch, share, 1)
    return (input_grad.reshape(blocks, rows, tokens), example_sketch)


def solution(mesh):
    in_specs = (
        P(None, "tensor", "groups"),
        P("groups", None),
        P(None, "tensor", None),
        P(),
        P(),
        P(),
        P(),
        P("groups"),
    )
    out_specs = (P(None, "tensor", "groups"), P("groups", "tensor"))
    return jax.shard_map(body, mesh=mesh, in_specs=in_specs, out_specs=out_specs, check_vma=False)
```

```python
import functools

import jax
import jax.numpy as jnp
from jax import lax
from jax.experimental import pallas as pl
from jax.experimental.pallas import tpu as pltpu
from jax.sharding import PartitionSpec as P

highest = lax.Precision.HIGHEST
MB = 1 << 20
BLOCK = 256
BF, F32 = jnp.bfloat16, jnp.float32


def parity_sign(first_ids, second_ids):
    common = first_ids & second_ids
    for shift in (8, 4, 2, 1):
        common = common ^ (common >> shift)
    return (1 - 2 * (common & 1)).astype(F32)


def iota(shape, dim):
    return lax.broadcasted_iota(jnp.int32, shape, dim)


def table():
    return parity_sign(iota((BLOCK, BLOCK), 0), iota((BLOCK, BLOCK), 1)).astype(BF)


def dot(a, b):
    return jnp.dot(a, b, preferred_element_type=F32)


def dot_nt(a, b):
    return lax.dot_general(a, b, (((1,), (1,)), ((), ())), preferred_element_type=F32)


def two_terms(x):
    hi = x.astype(BF)
    return hi, (x - hi.astype(F32)).astype(BF)


def butterflies(blocks):
    blocks = list(blocks)
    step = 1
    while step < len(blocks):
        for i in range(len(blocks)):
            if not i & step:
                a, b = blocks[i], blocks[i + step]
                blocks[i], blocks[i + step] = a + b, a - b
        step *= 2
    return blocks


def column(row, base, count):
    shape = (count, row.shape[1])
    wanted = iota(shape, 1) == iota(shape, 0) + base
    return jnp.sum(jnp.where(wanted, row.astype(F32), 0.0), axis=1, keepdims=True).astype(jnp.int32)


def hidden_share(me, picks, signs_ref, shape):
    blocks, rows, _ = shape
    length = signs_ref.shape[2]
    parts = length // BLOCK
    sketch = picks.shape[0]
    start = me * rows
    home = start // BLOCK
    pick_q = picks // length
    pick_r = picks % length
    chosen = (pick_q == iota((sketch, blocks), 1)).astype(F32).astype(BF)

    def sign_of(section, where):
        return 1.0 - 2.0 * dot(chosen, signs_ref[section, :, where].astype(F32).astype(BF))

    walsh = table()
    low = parity_sign(pick_r % BLOCK, iota((sketch, BLOCK), 1))
    high = pick_r // BLOCK
    first = []
    for c in range(parts):
        v = low * parity_sign(high, jnp.full_like(high, c)) * sign_of(2, pl.ds(c * BLOCK, BLOCK))
        first.append(dot(v.astype(BF), walsh))
    first = butterflies(first)
    total = None
    for c in range(parts):
        side = parity_sign(jnp.full((1, BLOCK), home, jnp.int32), jnp.full((1, BLOCK), c, jnp.int32))
        term = first[c] * (sign_of(1, pl.ds(c * BLOCK, BLOCK)) * side)
        total = term if total is None else total + term
    hi, lo = two_terms(total)
    second = dot(hi, walsh) + dot(lo, walsh)
    second = second * sign_of(0, pl.ds(pl.multiple_of(home * BLOCK, BLOCK), BLOCK))
    hi, lo = two_terms(second)
    if rows < BLOCK:
        pick_out = (iota((BLOCK, rows), 0) == iota((BLOCK, rows), 1) + (start - home * BLOCK)).astype(F32).astype(BF)
        hi = dot(hi, pick_out).astype(BF)
        lo = dot(lo, pick_out).astype(BF)
    return pick_q, hi, lo


def grad_share(picks, signs_ref, write):
    width = signs_ref.shape[1]
    parts = width // BLOCK
    walsh = table()
    low = parity_sign(picks % BLOCK, iota((8, BLOCK), 1))
    high = picks // BLOCK

    def sign_of(section, c):
        bits = signs_ref[section : section + 1, c * BLOCK : (c + 1) * BLOCK]
        return (1 - 2 * bits).astype(F32)

    def rows_of(x, c):
        return x[c * 8 : (c + 1) * 8]

    v = [low * parity_sign(high, jnp.full_like(high, c)) * sign_of(2, c) for c in range(parts)]
    first = dot(jnp.concatenate(v, axis=0).astype(BF), walsh)
    first = butterflies([rows_of(first, c) for c in range(parts)])
    first = jnp.concatenate([first[c] * sign_of(1, c) for c in range(parts)], axis=0)
    hi, lo = two_terms(first)
    second = dot(hi, walsh) + dot(lo, walsh)
    second = butterflies([rows_of(second, c) for c in range(parts)])
    for c in range(parts):
        x = second[c] * sign_of(0, c)
        h = x.astype(BF).astype(F32)
        write(c, jnp.concatenate([h, x - h], axis=0).astype(BF))


def kernel(
    n, keep, hp_ref, gp_ref, hs_hbm, gs_hbm, x_hbm, g_hbm, w_hbm, out_hbm, found_ref, grads_ref,
    hs_vm, gs_vm, x_vm, g_vm, w_first, w_vm, o_vm, part, send, recv, in_sem, g_sem, first_sem, w_sem, out_sem, send_sem, recv_sem,
):
    me = lax.axis_index("tensor")
    width = g_hbm.shape[1]
    tiles, bm, tokens = o_vm.shape
    blocks = x_hbm.shape[0]
    length = hs_hbm.shape[2]
    sketch = hp_ref.shape[1]
    pieces = sketch // keep
    chunks = g_sem.shape[0]
    span = width // chunks

    def fetch_w(t, slot):
        where = pl.ds(pl.multiple_of(t * bm, bm), bm)
        return pltpu.make_async_copy(w_hbm.at[where, :], w_vm.at[slot], w_sem.at[slot])

    def put_out(t):
        where = pl.ds(pl.multiple_of(t * bm, bm), bm)
        return pltpu.make_async_copy(o_vm.at[t], out_hbm.at[where, :], out_sem.at[t])

    def send_to(d):
        peer = lax.rem(me + d, n)
        return pltpu.make_async_remote_copy(
            src_ref=send.at[peer * pieces // n],
            dst_ref=recv.at[me],
            send_sem=send_sem.at[d],
            recv_sem=recv_sem.at[me],
            device_id={"tensor": peer},
            device_id_type=pl.DeviceIdType.MESH,
        )

    signs = [
        pltpu.make_async_copy(gs_hbm, gs_vm, in_sem.at[0]),
        pltpu.make_async_copy(hs_hbm, hs_vm, in_sem.at[1]),
    ]
    get_x = pltpu.make_async_copy(x_hbm, x_vm, in_sem.at[2])
    early = []
    for j in range(chunks):
        where = pl.ds(j * span, span)
        early.append(
            (
                pltpu.make_async_copy(g_hbm.at[:, where], g_vm.at[:, where], g_sem.at[j]),
                pltpu.make_async_copy(
                    w_hbm.at[pl.ds(0, bm), where], w_first.at[pl.ds(0, bm), where], first_sem.at[j]
                ),
            )
        )
    for copy in signs:
        copy.start()
    for pair in early:
        for copy in pair:
            copy.start()
    get_x.start()

    barrier = pltpu.get_barrier_semaphore()

    def greet(d, carry):
        pl.semaphore_signal(
            barrier, inc=1, device_id={"tensor": lax.rem(me + d, n)}, device_id_type=pl.DeviceIdType.MESH
        )
        return carry

    lax.fori_loop(1, n, greet, 0)

    signs[0].wait()

    def write(c, both):
        w_first[bm : bm + 16, c * BLOCK : (c + 1) * BLOCK] = both

    grad_share(column(gp_ref[...], me * pieces // n * keep, 8), gs_vm, write)
    signs[1].wait()
    pick_q, hi, lo = hidden_share(me, column(hp_ref[...], 0, sketch), hs_vm, x_hbm.shape)
    tall = None
    for j, pair in enumerate(early):
        for copy in pair:
            copy.wait()
        if j == 1 and tiles > 1:
            fetch_w(1, 0).start()
        where = slice(j * span, (j + 1) * span)
        term = dot_nt(w_first[:, where], g_vm[:, where])
        tall = term if tall is None else tall + term
    if tiles > 2:
        fetch_w(2, 1).start()
    o_vm[0] = tall[:bm].astype(BF)
    put_out(0).start()
    get_x.wait()
    total = None
    for q in range(blocks):
        own = pick_q == q
        both = jnp.concatenate([jnp.where(own, hi.astype(F32), 0.0), jnp.where(own, lo.astype(F32), 0.0)], axis=0)
        term = dot(both.astype(BF), x_vm[q])
        total = term if total is None else total + term
    part[...] = (total[:sketch] + total[sketch:]) * (length ** -1.5)
    own_grad = (tall[bm : bm + 8] + tall[bm + 8 : bm + 16]) * (width ** -1.5)
    rest = send.shape[1] - 2 * keep
    for p in range(pieces):
        rows = [part[p * keep : (p + 1) * keep, :], own_grad[:keep]]
        if rest:
            rows.append(jnp.zeros((rest, tokens), F32))
        send[p] = jnp.concatenate(rows, axis=0)
    recv[me] = send[me * pieces // n]
    pl.semaphore_wait(barrier, n - 1)

    def start_send(d, carry):
        send_to(d).start()
        return carry

    lax.fori_loop(1, n, start_send, 0)

    def one_tile(t, carry):
        slot = lax.rem(t - 1, 2)
        fetch_w(t, slot).wait()
        o_vm[t] = dot_nt(w_vm[slot], g_vm[...]).astype(BF)
        put_out(t).start()

        @pl.when(t + 2 < tiles)
        def _():
            fetch_w(t + 2, slot).start()

        return carry

    if tiles > 1:
        lax.fori_loop(1, tiles, one_tile, 0)

    def end_send(d, carry):
        send_to(d).wait_send()
        peer = lax.rem(me + d, n)
        pltpu.make_async_remote_copy(
            src_ref=send.at[0],
            dst_ref=recv.at[peer],
            send_sem=send_sem.at[d],
            recv_sem=recv_sem.at[peer],
            device_id={"tensor": peer},
            device_id_type=pl.DeviceIdType.MESH,
        ).wait_recv()
        return carry

    lax.fori_loop(1, n, end_send, 0)
    found = recv[0][:keep]
    for j in range(1, n):
        found = found + recv[j][:keep]
    found_ref[...] = found
    grads_ref[...] = jnp.concatenate([recv[p * n // pieces][keep : 2 * keep] for p in range(pieces)], axis=0)

    def end_out(t, carry):
        put_out(t).wait()
        return carry

    lax.fori_loop(0, tiles, end_out, 0)


def last_kernel(found_ref, grads_ref, len_ref, given, out_hbm, sk_ref, held, read_sem, write_sem):
    parts, rows, tokens = held.shape
    keep = found_ref.shape[0]
    seqs = len_ref.shape[1]
    seq_len = tokens // seqs
    reads = [pltpu.make_async_copy(given.at[pl.ds(j * rows, rows), :], held.at[j], read_sem.at[j]) for j in range(parts)]
    writes = [
        pltpu.make_async_copy(held.at[j], out_hbm.at[pl.ds(j * rows, rows), :], write_sem.at[j]) for j in range(parts)
    ]
    for copy in reads:
        copy.start()
    for copy, after in zip(reads, writes):
        copy.wait()
        after.start()
    lens = column(len_ref[...], 0, seqs)
    places = iota((seqs, tokens), 1)
    live = ((places // seq_len == iota((seqs, tokens), 0)) & (places % seq_len < lens)).astype(F32)
    left = jnp.concatenate([live * found_ref[a : a + 1, :] for a in range(keep)], axis=0)
    result = lax.dot_general(
        left, grads_ref[...], (((1,), (1,)), ((), ())), precision=highest, preferred_element_type=F32
    )
    sk_ref[...] = jnp.concatenate([result[a * seqs : (a + 1) * seqs] for a in range(keep)], axis=1)
    for copy in writes:
        copy.wait()


def body(hidden_in, out_grad, down_weight, hidden_signs, grad_signs, hidden_picks, grad_picks, seq_lengths):
    n = lax.axis_size("tensor")
    rank = lax.axis_index("tensor")
    blocks, rows, tokens = hidden_in.shape
    width = out_grad.shape[1]
    sketch = hidden_picks.shape[0]
    seqs = seq_lengths.shape[0]
    share = sketch * sketch // n
    keep = max(1, sketch // n)
    m = blocks * rows
    bm = BLOCK if m % BLOCK == 0 else m
    tiles = m // bm
    message = -(-2 * keep // 8) * 8
    flat_weight = down_weight.reshape(m, width)
    vmem = pl.BlockSpec(memory_space=pltpu.VMEM)
    hbm = pl.BlockSpec(memory_space=pl.ANY)
    dma = pltpu.SemaphoreType.DMA
    input_grad, found, grads = pl.pallas_call(
        functools.partial(kernel, n, keep),
        out_shape=(
            jax.ShapeDtypeStruct((m, tokens), BF),
            jax.ShapeDtypeStruct((keep, tokens), F32),
            jax.ShapeDtypeStruct((sketch, tokens), F32),
        ),
        in_specs=[vmem] * 2 + [hbm] * 5,
        out_specs=(hbm, vmem, vmem),
        scratch_shapes=[
            pltpu.VMEM(hidden_signs.shape, jnp.int32),
            pltpu.VMEM(grad_signs.shape, jnp.int32),
            pltpu.VMEM(hidden_in.shape, BF),
            pltpu.VMEM((tokens, width), BF),
            pltpu.VMEM((bm + 16, width), BF),
            pltpu.VMEM((2, bm, width), BF),
            pltpu.VMEM((tiles, bm, tokens), BF),
            pltpu.VMEM((sketch, tokens), F32),
            pltpu.VMEM((sketch // keep, message, tokens), F32),
            pltpu.VMEM((n, message, tokens), F32),
            dma((3,)),
            dma((4,)),
            dma((4,)),
            dma((2,)),
            dma((tiles,)),
            dma((n,)),
            dma((n,)),
        ],
        compiler_params=pltpu.CompilerParams(
            vmem_limit_bytes=56 * MB, collective_id=0, has_side_effects=True
        ),
        cost_estimate=pl.CostEstimate(
            flops=2 * m * tokens * width, bytes_accessed=2 * (m + tokens) * width, transcendentals=0
        ),
    )(
        hidden_picks.reshape(1, sketch),
        grad_picks.reshape(1, sketch),
        hidden_signs,
        grad_signs,
        hidden_in,
        out_grad,
        flat_weight,
    )
    input_grad, example_sketch = pl.pallas_call(
        last_kernel,
        out_shape=(
            jax.ShapeDtypeStruct((m, tokens), BF),
            jax.ShapeDtypeStruct((seqs, keep * sketch), F32),
        ),
        in_specs=[vmem] * 3 + [hbm],
        out_specs=(hbm, vmem),
        scratch_shapes=[pltpu.VMEM((tiles, bm, tokens), BF), dma((tiles,)), dma((tiles,))],
        compiler_params=pltpu.CompilerParams(vmem_limit_bytes=63 * MB),
    )(found, grads, seq_lengths.reshape(1, seqs), input_grad)
    if share < keep * sketch:
        example_sketch = lax.dynamic_slice_in_dim(example_sketch, rank * share % sketch, share, 1)
    return (input_grad.reshape(blocks, rows, tokens), example_sketch)


def solution(mesh):
    in_specs = (
        P(None, "tensor", "groups"),
        P("groups", None),
        P(None, "tensor", None),
        P(),
        P(),
        P(),
        P(),
        P("groups"),
    )
    out_specs = (P(None, "tensor", "groups"), P("groups", "tensor"))
    return jax.shard_map(body, mesh=mesh, in_specs=in_specs, out_specs=out_specs, check_vma=False)
```

```python
import functools

import jax
import jax.numpy as jnp
from jax import lax
from jax.experimental import pallas as pl
from jax.experimental.pallas import tpu as pltpu
from jax.sharding import PartitionSpec as P

highest = lax.Precision.HIGHEST
MB = 1 << 20
BLOCK = 256
BF, F32 = jnp.bfloat16, jnp.float32


def parity_sign(first_ids, second_ids):
    common = first_ids & second_ids
    for shift in (8, 4, 2, 1):
        common = common ^ (common >> shift)
    return (1 - 2 * (common & 1)).astype(F32)


def iota(shape, dim):
    return lax.broadcasted_iota(jnp.int32, shape, dim)


def table():
    return parity_sign(iota((BLOCK, BLOCK), 0), iota((BLOCK, BLOCK), 1)).astype(BF)


def dot(a, b):
    return jnp.dot(a, b, preferred_element_type=F32)


def dot_nt(a, b):
    return lax.dot_general(a, b, (((1,), (1,)), ((), ())), preferred_element_type=F32)


def two_terms(x):
    hi = x.astype(BF)
    return hi, (x - hi.astype(F32)).astype(BF)


def butterflies(blocks):
    blocks = list(blocks)
    step = 1
    while step < len(blocks):
        for i in range(len(blocks)):
            if not i & step:
                a, b = blocks[i], blocks[i + step]
                blocks[i], blocks[i + step] = a + b, a - b
        step *= 2
    return blocks


def column(row, base, count):
    shape = (count, row.shape[1])
    wanted = iota(shape, 1) == iota(shape, 0) + base
    return jnp.sum(jnp.where(wanted, row.astype(F32), 0.0), axis=1, keepdims=True).astype(jnp.int32)


def hidden_share(me, picks, signs_ref, shape):
    blocks, rows, _ = shape
    length = signs_ref.shape[2]
    parts = length // BLOCK
    sketch = picks.shape[0]
    start = me * rows
    home = start // BLOCK
    pick_q = picks // length
    pick_r = picks % length
    chosen = (pick_q == iota((sketch, blocks), 1)).astype(F32).astype(BF)

    def sign_of(section, where):
        return 1.0 - 2.0 * dot(chosen, signs_ref[section, :, where].astype(F32).astype(BF))

    walsh = table()
    low = parity_sign(pick_r % BLOCK, iota((sketch, BLOCK), 1))
    high = pick_r // BLOCK
    first = []
    for c in range(parts):
        v = low * parity_sign(high, jnp.full_like(high, c)) * sign_of(2, pl.ds(c * BLOCK, BLOCK))
        first.append(dot(v.astype(BF), walsh))
    first = butterflies(first)
    total = None
    for c in range(parts):
        side = parity_sign(jnp.full((1, BLOCK), home, jnp.int32), jnp.full((1, BLOCK), c, jnp.int32))
        term = first[c] * (sign_of(1, pl.ds(c * BLOCK, BLOCK)) * side)
        total = term if total is None else total + term
    hi, lo = two_terms(total)
    second = dot(hi, walsh) + dot(lo, walsh)
    second = second * sign_of(0, pl.ds(pl.multiple_of(home * BLOCK, BLOCK), BLOCK))
    hi, lo = two_terms(second)
    if rows < BLOCK:
        pick_out = (iota((BLOCK, rows), 0) == iota((BLOCK, rows), 1) + (start - home * BLOCK)).astype(F32).astype(BF)
        hi = dot(hi, pick_out).astype(BF)
        lo = dot(lo, pick_out).astype(BF)
    return pick_q, hi, lo


def grad_share(picks, signs_ref, write):
    width = signs_ref.shape[1]
    parts = width // BLOCK
    walsh = table()
    low = parity_sign(picks % BLOCK, iota((8, BLOCK), 1))
    high = picks // BLOCK

    def sign_of(section, c):
        bits = signs_ref[section : section + 1, c * BLOCK : (c + 1) * BLOCK]
        return (1 - 2 * bits).astype(F32)

    def rows_of(x, c):
        return x[c * 8 : (c + 1) * 8]

    v = [low * parity_sign(high, jnp.full_like(high, c)) * sign_of(2, c) for c in range(parts)]
    first = dot(jnp.concatenate(v, axis=0).astype(BF), walsh)
    first = butterflies([rows_of(first, c) for c in range(parts)])
    first = jnp.concatenate([first[c] * sign_of(1, c) for c in range(parts)], axis=0)
    hi, lo = two_terms(first)
    second = dot(hi, walsh) + dot(lo, walsh)
    second = butterflies([rows_of(second, c) for c in range(parts)])
    for c in range(parts):
        x = second[c] * sign_of(0, c)
        h = x.astype(BF).astype(F32)
        write(c, jnp.concatenate([h, x - h], axis=0).astype(BF))


def kernel(
    n, keep, hp_ref, gp_ref, hs_hbm, gs_hbm, x_hbm, g_hbm, w_hbm, out_hbm, found_ref, grads_ref,
    hs_vm, gs_vm, x_vm, g_vm, w_first, w_vm, o_vm, part, send, recv, in_sem, g_sem, first_sem, w_sem, out_sem, send_sem, recv_sem,
):
    me = lax.axis_index("tensor")
    width = g_hbm.shape[1]
    tiles, bm, tokens = o_vm.shape
    blocks = x_hbm.shape[0]
    length = hs_hbm.shape[2]
    sketch = hp_ref.shape[1]
    pieces = sketch // keep
    chunks = g_sem.shape[0]
    span = width // chunks

    def fetch_w(t, slot):
        where = pl.ds(pl.multiple_of(t * bm, bm), bm)
        return pltpu.make_async_copy(w_hbm.at[where, :], w_vm.at[slot], w_sem.at[slot])

    def put_out(t):
        where = pl.ds(pl.multiple_of(t * bm, bm), bm)
        return pltpu.make_async_copy(o_vm.at[t], out_hbm.at[where, :], out_sem.at[t])

    def send_to(d):
        peer = lax.rem(me + d, n)
        return pltpu.make_async_remote_copy(
            src_ref=send.at[peer * pieces // n],
            dst_ref=recv.at[me],
            send_sem=send_sem.at[d],
            recv_sem=recv_sem.at[me],
            device_id={"tensor": peer},
            device_id_type=pl.DeviceIdType.MESH,
        )

    signs = [
        pltpu.make_async_copy(gs_hbm, gs_vm, in_sem.at[0]),
        pltpu.make_async_copy(hs_hbm, hs_vm, in_sem.at[1]),
    ]
    get_x = pltpu.make_async_copy(x_hbm, x_vm, in_sem.at[2])
    early = []
    for j in range(chunks):
        where = pl.ds(j * span, span)
        early.append(
            (
                pltpu.make_async_copy(g_hbm.at[:, where], g_vm.at[:, where], g_sem.at[j]),
                pltpu.make_async_copy(
                    w_hbm.at[pl.ds(0, bm), where], w_first.at[pl.ds(0, bm), where], first_sem.at[j]
                ),
            )
        )
    for copy in signs:
        copy.start()
    for pair in early:
        for copy in pair:
            copy.start()
    get_x.start()

    barrier = pltpu.get_barrier_semaphore()

    def greet(d, carry):
        pl.semaphore_signal(
            barrier, inc=1, device_id={"tensor": lax.rem(me + d, n)}, device_id_type=pl.DeviceIdType.MESH
        )
        return carry

    lax.fori_loop(1, n, greet, 0)

    signs[0].wait()

    def write(c, both):
        w_first[bm : bm + 16, c * BLOCK : (c + 1) * BLOCK] = both

    grad_share(column(gp_ref[...], me * pieces // n * keep, 8), gs_vm, write)
    signs[1].wait()
    pick_q, hi, lo = hidden_share(me, column(hp_ref[...], 0, sketch), hs_vm, x_hbm.shape)
    tall = None
    for j, pair in enumerate(early):
        for copy in pair:
            copy.wait()
        if j == 1 and tiles > 1:
            fetch_w(1, 0).start()
        where = slice(j * span, (j + 1) * span)
        term = dot_nt(w_first[:, where], g_vm[:, where])
        tall = term if tall is None else tall + term
    if tiles > 2:
        fetch_w(2, 1).start()
    o_vm[0] = tall[:bm].astype(BF)
    put_out(0).start()
    get_x.wait()
    total = None
    for q in range(blocks):
        own = pick_q == q
        both = jnp.concatenate([jnp.where(own, hi.astype(F32), 0.0), jnp.where(own, lo.astype(F32), 0.0)], axis=0)
        term = dot(both.astype(BF), x_vm[q])
        total = term if total is None else total + term
    part[...] = (total[:sketch] + total[sketch:]) * (length ** -1.5)
    own_grad = (tall[bm : bm + 8] + tall[bm + 8 : bm + 16]) * (width ** -1.5)
    rest = send.shape[1] - 2 * keep
    for p in range(pieces):
        rows = [part[p * keep : (p + 1) * keep, :], own_grad[:keep]]
        if rest:
            rows.append(jnp.zeros((rest, tokens), F32))
        send[p] = jnp.concatenate(rows, axis=0)
    recv[me] = send[me * pieces // n]
    pl.semaphore_wait(barrier, n - 1)

    def start_send(d, carry):
        send_to(d).start()
        return carry

    lax.fori_loop(1, n, start_send, 0)

    def one_tile(t, carry):
        slot = lax.rem(t - 1, 2)
        fetch_w(t, slot).wait()
        o_vm[t] = dot_nt(w_vm[slot], g_vm[...]).astype(BF)
        put_out(t).start()

        @pl.when(t + 2 < tiles)
        def _():
            fetch_w(t + 2, slot).start()

        return carry

    if tiles > 1:
        lax.fori_loop(1, tiles, one_tile, 0)

    def end_send(d, carry):
        send_to(d).wait_send()
        peer = lax.rem(me + d, n)
        pltpu.make_async_remote_copy(
            src_ref=send.at[0],
            dst_ref=recv.at[peer],
            send_sem=send_sem.at[d],
            recv_sem=recv_sem.at[peer],
            device_id={"tensor": peer},
            device_id_type=pl.DeviceIdType.MESH,
        ).wait_recv()
        return carry

    lax.fori_loop(1, n, end_send, 0)
    found = recv[0][:keep]
    for j in range(1, n):
        found = found + recv[j][:keep]
    found_ref[...] = found
    grads_ref[...] = jnp.concatenate([recv[p * n // pieces][keep : 2 * keep] for p in range(pieces)], axis=0)

    def end_out(t, carry):
        put_out(t).wait()
        return carry

    lax.fori_loop(0, tiles, end_out, 0)


def last_kernel(
    found_hbm, grads_hbm, len_hbm, given, out_hbm, sk_hbm, found_ref, grads_ref, len_ref, sk_ref, held, small_sem, read_sem, write_sem
):
    parts, rows, tokens = held.shape
    keep = found_ref.shape[0]
    seqs = len_ref.shape[1]
    seq_len = tokens // seqs
    reads = [pltpu.make_async_copy(given.at[pl.ds(j * rows, rows), :], held.at[j], read_sem.at[j]) for j in range(parts)]
    writes = [
        pltpu.make_async_copy(held.at[j], out_hbm.at[pl.ds(j * rows, rows), :], write_sem.at[j]) for j in range(parts)
    ]
    small = [
        pltpu.make_async_copy(found_hbm, found_ref, small_sem.at[0]),
        pltpu.make_async_copy(grads_hbm, grads_ref, small_sem.at[1]),
        pltpu.make_async_copy(len_hbm, len_ref, small_sem.at[2]),
    ]
    put_sketch = pltpu.make_async_copy(sk_ref, sk_hbm, small_sem.at[3])
    for copy in small + reads:
        copy.start()
    for copy in small:
        copy.wait()
    for copy, after in zip(reads, writes):
        copy.wait()
        after.start()
    lens = column(len_ref[...], 0, seqs)
    places = iota((seqs, tokens), 1)
    live = ((places // seq_len == iota((seqs, tokens), 0)) & (places % seq_len < lens)).astype(F32)
    left = jnp.concatenate([live * found_ref[a : a + 1, :] for a in range(keep)], axis=0)
    result = lax.dot_general(
        left, grads_ref[...], (((1,), (1,)), ((), ())), precision=highest, preferred_element_type=F32
    )
    sk_ref[...] = jnp.concatenate([result[a * seqs : (a + 1) * seqs] for a in range(keep)], axis=1)
    put_sketch.start()
    for copy in writes:
        copy.wait()
    put_sketch.wait()


def body(hidden_in, out_grad, down_weight, hidden_signs, grad_signs, hidden_picks, grad_picks, seq_lengths):
    n = lax.axis_size("tensor")
    rank = lax.axis_index("tensor")
    blocks, rows, tokens = hidden_in.shape
    width = out_grad.shape[1]
    sketch = hidden_picks.shape[0]
    seqs = seq_lengths.shape[0]
    share = sketch * sketch // n
    keep = max(1, sketch // n)
    m = blocks * rows
    bm = BLOCK if m % BLOCK == 0 else m
    tiles = m // bm
    message = -(-2 * keep // 8) * 8
    flat_weight = down_weight.reshape(m, width)
    vmem = pl.BlockSpec(memory_space=pltpu.VMEM)
    hbm = pl.BlockSpec(memory_space=pl.ANY)
    dma = pltpu.SemaphoreType.DMA
    input_grad, found, grads = pl.pallas_call(
        functools.partial(kernel, n, keep),
        out_shape=(
            jax.ShapeDtypeStruct((m, tokens), BF),
            jax.ShapeDtypeStruct((keep, tokens), F32),
            jax.ShapeDtypeStruct((sketch, tokens), F32),
        ),
        in_specs=[vmem] * 2 + [hbm] * 5,
        out_specs=(hbm, vmem, vmem),
        scratch_shapes=[
            pltpu.VMEM(hidden_signs.shape, jnp.int32),
            pltpu.VMEM(grad_signs.shape, jnp.int32),
            pltpu.VMEM(hidden_in.shape, BF),
            pltpu.VMEM((tokens, width), BF),
            pltpu.VMEM((bm + 16, width), BF),
            pltpu.VMEM((2, bm, width), BF),
            pltpu.VMEM((tiles, bm, tokens), BF),
            pltpu.VMEM((sketch, tokens), F32),
            pltpu.VMEM((sketch // keep, message, tokens), F32),
            pltpu.VMEM((n, message, tokens), F32),
            dma((3,)),
            dma((4,)),
            dma((4,)),
            dma((2,)),
            dma((tiles,)),
            dma((n,)),
            dma((n,)),
        ],
        compiler_params=pltpu.CompilerParams(
            vmem_limit_bytes=56 * MB, collective_id=0, has_side_effects=True
        ),
        cost_estimate=pl.CostEstimate(
            flops=2 * m * tokens * width, bytes_accessed=2 * (m + tokens) * width, transcendentals=0
        ),
    )(
        hidden_picks.reshape(1, sketch),
        grad_picks.reshape(1, sketch),
        hidden_signs,
        grad_signs,
        hidden_in,
        out_grad,
        flat_weight,
    )
    input_grad, example_sketch = pl.pallas_call(
        last_kernel,
        out_shape=(
            jax.ShapeDtypeStruct((m, tokens), BF),
            jax.ShapeDtypeStruct((seqs, keep * sketch), F32),
        ),
        in_specs=[hbm] * 4,
        out_specs=(hbm, hbm),
        scratch_shapes=[
            pltpu.VMEM((keep, tokens), F32),
            pltpu.VMEM((sketch, tokens), F32),
            pltpu.VMEM((1, seqs), jnp.int32),
            pltpu.VMEM((seqs, keep * sketch), F32),
            pltpu.VMEM((tiles, bm, tokens), BF),
            dma((4,)),
            dma((tiles,)),
            dma((tiles,)),
        ],
        compiler_params=pltpu.CompilerParams(vmem_limit_bytes=63 * MB),
    )(found, grads, seq_lengths.reshape(1, seqs), input_grad)
    if share < keep * sketch:
        example_sketch = lax.dynamic_slice_in_dim(example_sketch, rank * share % sketch, share, 1)
    return (input_grad.reshape(blocks, rows, tokens), example_sketch)


def solution(mesh):
    in_specs = (
        P(None, "tensor", "groups"),
        P("groups", None),
        P(None, "tensor", None),
        P(),
        P(),
        P(),
        P(),
        P("groups"),
    )
    out_specs = (P(None, "tensor", "groups"), P("groups", "tensor"))
    return jax.shard_map(body, mesh=mesh, in_specs=in_specs, out_specs=out_specs, check_vma=False)
```
